256 devices in a mesh: pipe: 8 (over z), sp: 16 (over y_hi, x, core), cfg: 2 (over y_lo).
Axes of the slice: x: 4, y: 4 (y_hi: 2, y_lo: 2; y = y_hi * 2 + y_lo), z: 8, core: 2. Of those that a mesh axis runs over, the one named last changes fastest.
Arguments:
- patch_tokens: bfloat16 [4, 128, 3072], P(None, 'sp'), may hold values from -6 to 6
- modulation: float32 [8, 2, 3, 3072], P('pipe', 'cfg'), may hold values from -3 to 3
- w_qkv: bfloat16 [8, 3072, 3, 2048], P('pipe', None, None, 'sp'), may hold values from -1 to 1
- qk_gain: float32 [8, 2, 128], P('pipe'), may hold values from 0.5 to 8
- w_out: bfloat16 [8, 2048, 3072], P('pipe', 'sp'), may hold values from -0.125 to 0.125
- kv_cache: bfloat16 [8, 2, 2, 8192, 2048], P('pipe', 'cfg', None, None, 'sp'), may hold values from -6 to 6
- order: int32 [64], replicated, may hold values from 0 to 63, each once
- offsets: int32 [64], replicated, may hold values from 0 to 8064, as said below
Outputs:
- section_out: bfloat16 [8, 2, 4, 128, 3072], P('pipe', 'cfg', None, 'sp')
- guided: bfloat16 [4, 128, 3072], P('cfg', 'sp', 'pipe')
The draws below stay inside these ranges and needn't reach their ends.
Inputs may be any that keep to these rules, and one draw needn't show every extreme that they name: `order`: the first 4 entries name the window's patches. `offsets`: distinct multiples of 128, one for each image patch.
All inputs are finite; a program needn't handle non-finite values.
Results may differ from the reference program's by a relative error of at most 0.035.
Values may be sent and summed in bfloat16 or wider, within the bound.
No kernel may reach another device: no remote copies, remote signals or barrier semaphores. Data moves between devices by JAX's collectives and lax.ppermute only.
A program may use at most 128 MiB of HBM per device.

```python
import math
import jax
import jax.numpy as jnp
from jax import lax

D = 3072
HEADS = 16
HD = 128
PT = 128
NWIN = 4
L = 8192
NPATCH = 64
N_PIPE = 8
N_CFG = 2


def draw_w_qkv(key, part):
    key = jax.random.fold_in(key, 11)
    key_query, key_key, key_value = jax.random.split(key, 3)
    full_shape = (N_PIPE, D, HEADS * HD)
    factor = D ** (-0.5)
    queries = jax.random.normal(key_query, full_shape, jnp.float32) * factor
    keys_part = jax.random.normal(key_key, full_shape, jnp.float32) * factor
    values_part = jax.random.normal(key_value, full_shape, jnp.float32) * factor
    return jnp.stack([queries, keys_part, values_part], axis=2).astype(jnp.bfloat16)


def draw_qk_gain(key, part):
    key = jax.random.fold_in(key, 23)
    lowest = 0.5
    highest = 2.0
    logs = jax.random.uniform(key, (N_PIPE, 2, HD), jnp.float32, math.log(lowest), math.log(highest))
    return jnp.exp(logs).astype(jnp.float32)


def draw_offsets(key, part):
    key = jax.random.fold_in(key, 37)
    return (jax.random.permutation(key, NPATCH) * PT).astype(jnp.int32)


def steps_of(rng, extent, shards, low, top_value):
    factor_of, own = 1.0, jax.random.fold_in(rng, 6)
    for axis_at, shards_of in shards:
        heights = jnp.exp(jax.random.uniform(jax.random.fold_in(own, axis_at), (shards_of,), jnp.float32, low / len(shards), top_value / len(shards)))
        factor_of = factor_of * jnp.repeat(heights, extent[axis_at] // shards_of).reshape([-1 if axis == axis_at else 1 for axis in range(len(extent))])
    return factor_of


def gaussian(rng, extent, width, limit, shards=(), kind=jnp.bfloat16):
    values = jax.random.normal(rng, extent, jnp.float32) * width
    if len(shards) > 0:
        values = steps_of(rng, extent, shards, -0.22, 0.18) * values
    return jnp.clip(values, min=-limit, max=limit).astype(kind)


def setup_inputs(seed: int = 0) -> dict:
    splits = jax.random.split(jax.random.key(seed), 9)
    patch_tokens = gaussian(splits[0], (NWIN, PT, D), 1.0, 6.0, ((1, 16),))
    modulation = gaussian(splits[1], (N_PIPE, N_CFG, 3, D), 0.5, 3.0, ((0, 8), (1, 2)), jnp.float32)
    w_qkv = draw_w_qkv(jax.random.fold_in(splits[8], 71), 0)
    qk_gain = draw_qk_gain(jax.random.fold_in(splits[8], 71), 0)
    w_out = gaussian(splits[4], (N_PIPE, HEADS * HD, D), (HEADS * HD) ** -0.5, 0.125, ((0, 8), (1, 16)))
    kv_cache = gaussian(splits[5], (N_PIPE, N_CFG, 2, L, HEADS * HD), 1.0, 6.0, ((0, 8), (1, 2), (4, 16)))
    order = jax.random.permutation(splits[6], NPATCH).astype(jnp.int32)
    offsets = draw_offsets(jax.random.fold_in(splits[8], 71), 0)
    return {"patch_tokens": patch_tokens, "modulation": modulation, "w_qkv": w_qkv, "qk_gain": qk_gain, "w_out": w_out, "kv_cache": kv_cache, "order": order, "offsets": offsets}


norm_eps = 1e-06
guide_scale = 3.5

def layer_norm(tokens_in):
    centred = tokens_in - lax.optimization_barrier(jnp.mean(tokens_in, axis=-1, keepdims=True))
    spread_sq = lax.optimization_barrier(jnp.mean(centred * centred, axis=-1, keepdims=True))
    return centred * lax.rsqrt(spread_sq + norm_eps)

def head_norm(heads_in, gain_row):
    power = lax.optimization_barrier(jnp.mean(heads_in * heads_in, axis=-1, keepdims=True))
    return (heads_in * lax.rsqrt(power + norm_eps) * gain_row).astype(jnp.bfloat16)

def section(hidden, modulate, weight_in, gain_pair, weight_out, cache_keys, cache_values, row_start):
    row_count = hidden.shape[0]
    normed = layer_norm(hidden.astype(jnp.float32))
    modded = (normed * (1.0 + modulate[1]) + modulate[0]).astype(jnp.bfloat16)
    projected = jnp.dot(modded, weight_in.reshape(weight_in.shape[0], -1), preferred_element_type=jnp.float32)
    projected = projected.reshape(row_count, 3, HEADS, HD)
    queries = head_norm(projected[:, 0], gain_pair[0])
    fresh_keys = head_norm(projected[:, 1], gain_pair[1])
    fresh_values = projected[:, 2].astype(jnp.bfloat16)
    zero_col = jnp.zeros((), jnp.int32)
    start_row = row_start.astype(jnp.int32)
    all_keys = lax.dynamic_update_slice(cache_keys, fresh_keys.reshape(row_count, HEADS * HD), (start_row, zero_col))
    all_values = lax.dynamic_update_slice(cache_values, fresh_values.reshape(row_count, HEADS * HD), (start_row, zero_col))
    key_heads = all_keys.reshape(L, HEADS, HD).astype(jnp.float32)
    value_heads = all_values.reshape(L, HEADS, HD).astype(jnp.float32)
    scores = jnp.einsum('qhd,khd->hqk', queries.astype(jnp.float32), key_heads) / math.sqrt(HD)
    top_score = lax.optimization_barrier(jnp.max(scores, axis=-1, keepdims=True))
    weights = jnp.exp(scores - top_score)
    totals = lax.optimization_barrier(jnp.sum(weights, axis=-1))
    rounded = lax.optimization_barrier(weights.astype(jnp.bfloat16)).astype(jnp.float32)
    mixed_sum = jnp.einsum('hqk,khd->qhd', rounded, value_heads)
    attended = (mixed_sum / jnp.transpose(totals)[:, :, None]).astype(jnp.bfloat16)
    head_total = jnp.dot(attended.reshape(row_count, HEADS * HD), weight_out, preferred_element_type=jnp.float32)
    return (hidden.astype(jnp.float32) + modulate[2] * head_total).astype(jnp.bfloat16)

def reference(patch_tokens, modulation, w_qkv, qk_gain, w_out, kv_cache, order, offsets):
    section_out = jnp.zeros((N_PIPE, N_CFG, NWIN, PT, D), jnp.bfloat16)
    for branch in range(N_CFG):
        for patch_item in range(NWIN):
            row_start = offsets[order[patch_item]]
            hidden = patch_tokens[patch_item]
            for section_id in range(N_PIPE):
                hidden = section(hidden, modulation[section_id, branch], w_qkv[section_id], qk_gain[section_id], w_out[section_id], kv_cache[section_id, branch, 0], kv_cache[section_id, branch, 1], row_start)
                section_out = section_out.at[section_id, branch, patch_item].set(hidden)
    cond_rows = section_out[N_PIPE - 1, 0].astype(jnp.float32)
    uncond = section_out[N_PIPE - 1, 1].astype(jnp.float32)
    guided = (uncond + guide_scale * (cond_rows - uncond)).astype(jnp.bfloat16)
    return (section_out, guided)
```

```python
import functools
import math

import jax
import jax.numpy as jnp
from jax import lax
from jax.experimental import pallas as pl
from jax.experimental.pallas import tpu as pltpu
from jax.sharding import PartitionSpec as P

HD = 128
norm_eps = 1e-06
guide_scale = 3.5
CHUNK = 2048
WIDE = 512
SCALE = math.log2(math.e) / math.sqrt(HD)
VMEM_BYTES = 34 * 1024 * 1024


def dot(a, b):
    return jnp.dot(a, b, preferred_element_type=jnp.float32)


def dot_t(a, b):
    return lax.dot_general(a, b, (((1,), (1,)), ((), ())), preferred_element_type=jnp.float32)


def head_norm(heads_in, gain_row):
    power = jnp.mean(heads_in * heads_in, axis=-1, keepdims=True)
    return (heads_in * lax.rsqrt(power + norm_eps) * gain_row).astype(jnp.bfloat16)


def lanes_sum(total, wide):
    for b in range(wide.shape[1] // 128):
        total = total + wide[:, b * 128 : (b + 1) * 128]
    return total


def front_half(gathered, hidden_before, gate, w_out, entering, use_entering, hidden_out):
    rows, width = hidden_out.shape
    attended = jnp.concatenate([gathered[i] for i in range(gathered.shape[0])], axis=1)
    total = jnp.zeros((rows, 128), jnp.float32)
    for n in range(width // WIDE):
        cols = slice(n * WIDE, (n + 1) * WIDE)
        head_total = dot(attended, w_out[:, cols])
        before = hidden_before[:, cols].astype(jnp.float32)
        hidden = (before + gate[0:1, cols] * head_total).astype(jnp.bfloat16)
        if entering is not None:
            hidden = jnp.where(use_entering, entering[:, cols], hidden)
        hidden_out[:, cols] = hidden
        total = lanes_sum(total, hidden.astype(jnp.float32))
    return total


def back_half(
    total, hidden, modulate, w_own, w_other, gain, kv_own, kv_other, row_start, core, out, modded, scores
):
    rows, width = hidden.shape
    length = kv_own.shape[1]
    mean = jnp.sum(total, axis=1, keepdims=True) * (1.0 / width)
    spread = jnp.zeros((rows, 128), jnp.float32)
    for n in range(width // 128):
        centred = hidden[:, n * 128 : (n + 1) * 128].astype(jnp.float32) - mean
        spread = spread + centred * centred
    inverse = lax.rsqrt(jnp.sum(spread, axis=1, keepdims=True) * (1.0 / width) + norm_eps)
    for n in range(width // WIDE):
        cols = slice(n * WIDE, (n + 1) * WIDE)
        normed = (hidden[:, cols].astype(jnp.float32) - mean) * inverse
        modded[:, cols] = (normed * (1.0 + modulate[1:2, cols]) + modulate[0:1, cols]).astype(jnp.bfloat16)
    queries, fresh_keys, fresh_values = [], [], []
    for weight in (w_own, w_other):
        projected = dot(modded[...], weight[...])
        queries.append(head_norm(projected[:, :HD], gain[0:1, :]))
        fresh_keys.append(head_norm(projected[:, HD : 2 * HD], gain[1:2, :]))
        fresh_values.append(projected[:, 2 * HD :].astype(jnp.bfloat16))
    caches = (kv_own, kv_other)
    window = pl.ds(row_start, rows)
    window_block = lax.div(row_start, 128)
    steps = length // CHUNK
    lowest = jnp.full((rows, 128), -jnp.inf, jnp.float32)

    def score(head, step, top):
        part = slice(step * CHUNK, (step + 1) * CHUNK)
        old = dot_t(queries[head], caches[head][0, part, :])
        scores[head, :, part] = old
        for b in range(CHUNK // 128):
            replaced = step * (CHUNK // 128) + b == window_block
            top = jnp.maximum(top, jnp.where(replaced, -jnp.inf, old[:, b * 128 : (b + 1) * 128]))
        return top

    def start_weights(head, top):
        fresh = dot_t(queries[head], fresh_keys[head])
        scores[head, :, window] = lowest
        top = jnp.max(jnp.maximum(top, fresh), axis=1, keepdims=True)
        weights = jnp.exp2((fresh - top) * SCALE)
        return top, weights, dot(weights.astype(jnp.bfloat16), fresh_values[head])

    def weigh(head, step, top, totals, mixed):
        part = slice(step * CHUNK, (step + 1) * CHUNK)
        weights = jnp.exp2((scores[head, :, part] - top) * SCALE)
        totals = lanes_sum(totals, weights)
        return totals, mixed + dot(weights.astype(jnp.bfloat16), caches[head][1, part, :])

    top = lowest
    for step in range(steps):
        top = score(0, step, top)
    for head in range(2):
        top, totals, mixed = start_weights(head, top)
        next_top = lowest
        for step in range(steps):
            if head == 0:
                next_top = score(1, step, next_top)
            totals, mixed = weigh(head, step, top, totals, mixed)
        place = core if head == 0 else 1 - core
        cols = pl.ds(pl.multiple_of(place * HD, HD), HD)
        out[:, cols] = (mixed / jnp.sum(totals, axis=1, keepdims=True)).astype(jnp.bfloat16)
        top = next_top


def first_kernel(scal, x, mod, w_own, w_other, gain, kv_own, kv_other, out, modded, scores):
    total = jnp.zeros((x.shape[0], 128), jnp.float32)
    total = lanes_sum(total, x[...].astype(jnp.float32))
    back_half(
        total, x, mod, w_own, w_other, gain, kv_own, kv_other,
        pl.multiple_of(scal[0], 128), scal[1], out, modded, scores,
    )


def whole_kernel(has_x, scal, gathered, before, gate, w_out, *rest):
    x = rest[0] if has_x else None
    mod, w_own, w_other, gain, kv_own, kv_other, hidden, out, modded, scores = rest[has_x:]
    total = front_half(gathered, before, gate, w_out, x, scal[2] == 1, hidden)
    back_half(
        total, hidden, mod, w_own, w_other, gain, kv_own, kv_other,
        pl.multiple_of(scal[0], 128), scal[1], out, modded, scores,
    )


def last_kernel(gathered, before, gate, w_out, hidden):
    front_half(gathered, before, gate, w_out, None, None, hidden)


def call(kernel, operands, outs, scratch, scalars):
    vmem = pl.BlockSpec(memory_space=pltpu.VMEM)
    specs = [vmem] * len(operands)
    if scalars:
        specs[0] = pl.BlockSpec(memory_space=pltpu.SMEM)
    return pl.pallas_call(
        kernel,
        out_shape=outs,
        in_specs=specs,
        out_specs=tuple(vmem for _ in outs),
        scratch_shapes=scratch,
        compiler_params=pltpu.CompilerParams(vmem_limit_bytes=VMEM_BYTES),
    )(*operands)


def keep(array):
    return pltpu.with_memory_space_constraint(array, pltpu.VMEM)


def shards(patch_tokens, modulation, w_qkv, qk_gain, w_out, kv_cache, order, offsets):
    sections = lax.axis_size("pipe")
    members = lax.axis_size("sp")
    chips = members // 2
    section = lax.axis_index("pipe")
    place = lax.axis_index("sp")
    core = place % 2
    chip = place // 2
    window, own_rows, width = patch_tokens.shape
    slots = window // 2
    rows = own_rows * members
    bf16 = jnp.bfloat16

    same_core = [[2 * i + c for i in range(chips)] for c in range(2)]

    def other_core(value):
        return lax.ppermute(value, "sp", [(i, i ^ 1) for i in range(members)])

    def onward(value):
        return lax.ppermute(value, "pipe", [(i, (i + 1) % sections) for i in range(sections)])

    def back(value):
        return lax.ppermute(value, "pipe", [(i, (i - 1) % sections) for i in range(sections)])

    w_before = onward(w_out[0])
    gate_before = onward(modulation[0, 0, 2:3])
    kv_own = kv_cache[0, 0]
    kv_other = other_core(kv_own)
    w_own = w_qkv[0].reshape(width, 3 * HD)
    w_other = other_core(w_own)
    mod = modulation[0, 0, 0:2]
    gain = qk_gain[0]

    to_cores = jnp.swapaxes(patch_tokens.reshape(slots, 2, own_rows, width), 0, 1)
    to_all = jnp.broadcast_to(to_cores[None], (chips, 2, slots, own_rows, width))
    entered = lax.all_to_all(
        to_all.reshape(members, slots, own_rows, width), "sp", 0, 0, tiled=True
    )
    entering = [entered[:, k].reshape(rows, width) for k in range(slots)]

    w_all = lax.all_gather(w_before, "sp", axis=0, tiled=True)

    def start_of(patch):
        chosen = jnp.sum(jnp.where(jnp.arange(order.shape[0]) == patch, order, 0))
        return jnp.sum(jnp.where(jnp.arange(offsets.shape[0]) == chosen, offsets, 0))

    starts = [start_of(2 * k + core).astype(jnp.int32) for k in range(slots)]

    def scalars(tick):
        start = starts[0]
        for k in range(1, slots):
            start = jnp.where(tick - section >= k, starts[k], start)
        enters = (section == 0) & (tick < slots)
        return jnp.stack([start, core.astype(jnp.int32), enters.astype(jnp.int32)])

    statics = [mod, keep(w_own), keep(w_other), gain, keep(kv_own), keep(kv_other)]
    w_all = keep(w_all)
    hidden_shape = jax.ShapeDtypeStruct((rows, width), bf16)
    attended_shape = jax.ShapeDtypeStruct((rows, 2 * HD), bf16)
    scratch = [
        pltpu.VMEM((rows, width), bf16),
        pltpu.VMEM((2, rows, kv_own.shape[1]), jnp.float32),
    ]

    stored = [jnp.zeros((2 * own_rows, width), bf16) for _ in range(slots)]
    hidden = entering[0]
    (attended,) = call(
        first_kernel, [scalars(0), hidden, *statics], (attended_shape,), scratch, True
    )
    ticks = sections + slots
    for tick in range(1, ticks):
        arrived = onward(attended)
        before = onward(hidden)
        gathered = lax.all_to_all(
            jnp.broadcast_to(arrived[None], (chips, rows, 2 * HD)),
            "sp", 0, 0, axis_index_groups=same_core, tiled=True,
        )
        if tick == ticks - 1:
            (hidden,) = call(
                last_kernel, [gathered, before, gate_before, w_all], (hidden_shape,), [], False
            )
        else:
            has_x = tick < slots
            extra = [entering[tick]] if has_x else []
            hidden, attended = call(
                functools.partial(whole_kernel, has_x),
                [scalars(tick), gathered, before, gate_before, w_all, *extra, *statics],
                (hidden_shape, attended_shape), scratch, True,
            )
        chip_rows = lax.dynamic_slice_in_dim(hidden, chip * 2 * own_rows, 2 * own_rows, 0)
        ends = jnp.where(section == 0, sections, section)
        for k in range(slots):
            stored[k] = jnp.where(tick == ends + k, chip_rows, stored[k])

    both = jnp.stack(stored).reshape(slots, 2, own_rows, width)
    mine = jnp.where(core == 0, both[:, 0], both[:, 1])
    theirs = other_core(jnp.where(core == 0, both[:, 1], both[:, 0]))
    pair = jnp.where(core == 0, jnp.stack([mine, theirs], 1), jnp.stack([theirs, mine], 1))
    finished = pair.reshape(window, own_rows, width)
    section_out = back(finished)

    branches = lax.axis_size("cfg")
    part = width // sections
    pieces = finished.reshape(branches, window // branches, own_rows, sections, part)
    pieces = jnp.transpose(pieces, (3, 0, 1, 2, 4))
    pieces = pieces.reshape(sections * branches, window // branches, own_rows, part)
    landed = lax.all_to_all(pieces, ("pipe", "cfg"), 0, 0, tiled=True)
    cond = landed[0].astype(jnp.float32)
    uncond = landed[1].astype(jnp.float32)
    guided = (uncond + guide_scale * (cond - uncond)).astype(bf16)
    return (section_out[None, None], guided)


def solution(mesh):
    return jax.shard_map(
        shards,
        mesh=mesh,
        in_specs=(
            P(None, "sp", None),
            P("pipe", "cfg", None, None),
            P("pipe", None, None, "sp"),
            P("pipe", None, None),
            P("pipe", "sp", None),
            P("pipe", "cfg", None, None, "sp"),
            P(),
            P(),
        ),
        out_specs=(P("pipe", "cfg", None, "sp", None), P("cfg", "sp", "pipe")),
        check_vma=False,
    )
```

```python
import functools
import math

import jax
import jax.numpy as jnp
from jax import lax
from jax.experimental import pallas as pl
from jax.experimental.pallas import tpu as pltpu
from jax.sharding import PartitionSpec as P

HD = 128
norm_eps = 1e-06
guide_scale = 3.5
CHUNK = 2048
WIDE = 512
SCALE = math.log2(math.e) / math.sqrt(HD)
VMEM_BYTES = 20 * 1024 * 1024


def dot(a, b):
    return jnp.dot(a, b, preferred_element_type=jnp.float32)


def dot_t(a, b):
    return lax.dot_general(a, b, (((1,), (1,)), ((), ())), preferred_element_type=jnp.float32)


def head_norm(heads_in, gain_row):
    power = jnp.mean(heads_in * heads_in, axis=-1, keepdims=True)
    return (heads_in * lax.rsqrt(power + norm_eps) * gain_row).astype(jnp.bfloat16)


def lanes_sum(total, wide):
    for b in range(wide.shape[1] // 128):
        total = total + wide[:, b * 128 : (b + 1) * 128]
    return total


def front_half(gathered, hidden_before, gate, w_out, entering, use_entering, hidden_out):
    rows, width = hidden_out.shape
    attended = jnp.concatenate([gathered[i] for i in range(gathered.shape[0])], axis=1)
    total = jnp.zeros((rows, 128), jnp.float32)
    for n in range(width // WIDE):
        cols = slice(n * WIDE, (n + 1) * WIDE)
        head_total = dot(attended, w_out[:, cols])
        before = hidden_before[:, cols].astype(jnp.float32)
        hidden = (before + gate[0:1, cols] * head_total).astype(jnp.bfloat16)
        if entering is not None:
            hidden = jnp.where(use_entering, entering[:, cols], hidden)
        hidden_out[:, cols] = hidden
        total = lanes_sum(total, hidden.astype(jnp.float32))
    return total


def back_half(
    total, hidden, modulate, w_own, w_other, gain, kv_own, kv_other, row_start, core, out, modded, scores
):
    rows, width = hidden.shape
    length = kv_own.shape[1]
    mean = jnp.sum(total, axis=1, keepdims=True) * (1.0 / width)
    spread = jnp.zeros((rows, 128), jnp.float32)
    for n in range(width // 128):
        centred = hidden[:, n * 128 : (n + 1) * 128].astype(jnp.float32) - mean
        spread = spread + centred * centred
    inverse = lax.rsqrt(jnp.sum(spread, axis=1, keepdims=True) * (1.0 / width) + norm_eps)
    for n in range(width // WIDE):
        cols = slice(n * WIDE, (n + 1) * WIDE)
        normed = (hidden[:, cols].astype(jnp.float32) - mean) * inverse
        modded[:, cols] = (normed * (1.0 + modulate[1:2, cols]) + modulate[0:1, cols]).astype(jnp.bfloat16)
    queries, fresh_keys, fresh_values = [], [], []
    for weight in (w_own, w_other):
        projected = dot(modded[...], weight[...])
        queries.append(head_norm(projected[:, :HD], gain[0:1, :]))
        fresh_keys.append(head_norm(projected[:, HD : 2 * HD], gain[1:2, :]))
        fresh_values.append(projected[:, 2 * HD :].astype(jnp.bfloat16))
    caches = (kv_own, kv_other)
    window = pl.ds(row_start, rows)
    window_block = lax.div(row_start, 128)
    steps = length // CHUNK
    lowest = jnp.full((rows, 128), -jnp.inf, jnp.float32)

    def score(head, step, top):
        part = slice(step * CHUNK, (step + 1) * CHUNK)
        old = dot_t(queries[head], caches[head][0, part, :])
        scores[head, :, part] = old
        for b in range(CHUNK // 128):
            replaced = step * (CHUNK // 128) + b == window_block
            top = jnp.maximum(top, jnp.where(replaced, -jnp.inf, old[:, b * 128 : (b + 1) * 128]))
        return top

    def start_weights(head, top):
        fresh = dot_t(queries[head], fresh_keys[head])
        scores[head, :, window] = lowest
        top = jnp.max(jnp.maximum(top, fresh), axis=1, keepdims=True)
        weights = jnp.exp2((fresh - top) * SCALE)
        return top, weights, dot(weights.astype(jnp.bfloat16), fresh_values[head])

    def weigh(head, step, top, totals, mixed):
        part = slice(step * CHUNK, (step + 1) * CHUNK)
        weights = jnp.exp2((scores[head, :, part] - top) * SCALE)
        totals = lanes_sum(totals, weights)
        return totals, mixed + dot(weights.astype(jnp.bfloat16), caches[head][1, part, :])

    top = lowest
    for step in range(steps):
        top = score(0, step, top)
    for head in range(2):
        top, totals, mixed = start_weights(head, top)
        next_top = lowest
        for step in range(steps):
            if head == 0:
                next_top = score(1, step, next_top)
            totals, mixed = weigh(head, step, top, totals, mixed)
        place = core if head == 0 else 1 - core
        cols = pl.ds(pl.multiple_of(place * HD, HD), HD)
        out[:, cols] = (mixed / jnp.sum(totals, axis=1, keepdims=True)).astype(jnp.bfloat16)
        top = next_top


def first_kernel(tick, scal, x, mod, w_own, w_other, gain, kv_own, kv_other, out, modded, scores):
    total = jnp.zeros((x.shape[0], 128), jnp.float32)
    total = lanes_sum(total, x[...].astype(jnp.float32))
    back_half(
        total, x, mod, w_own, w_other, gain, kv_own, kv_other,
        pl.multiple_of(scal[2 + tick], 128), scal[0], out, modded, scores,
    )


def whole_kernel(tick, has_x, scal, gathered, before, gate, w_out, *rest):
    x = rest[0] if has_x else None
    mod, w_own, w_other, gain, kv_own, kv_other, hidden, out, modded, scores = rest[has_x:]
    total = front_half(gathered, before, gate, w_out, x, scal[1] == 0, hidden)
    back_half(
        total, hidden, mod, w_own, w_other, gain, kv_own, kv_other,
        pl.multiple_of(scal[2 + tick], 128), scal[0], out, modded, scores,
    )


def last_kernel(gathered, before, gate, w_out, hidden):
    front_half(gathered, before, gate, w_out, None, None, hidden)


def call(kernel, operands, outs, scratch, scalars):
    vmem = pl.BlockSpec(memory_space=pltpu.VMEM)
    specs = [vmem] * len(operands)
    if scalars:
        specs[0] = pl.BlockSpec(memory_space=pltpu.SMEM)
    return pl.pallas_call(
        kernel,
        out_shape=outs,
        in_specs=specs,
        out_specs=tuple(vmem for _ in outs),
        scratch_shapes=scratch,
        compiler_params=pltpu.CompilerParams(vmem_limit_bytes=VMEM_BYTES),
    )(*operands)


def keep(array):
    return pltpu.with_memory_space_constraint(array, pltpu.VMEM)


def shards(patch_tokens, modulation, w_qkv, qk_gain, w_out, kv_cache, order, offsets):
    sections = lax.axis_size("pipe")
    members = lax.axis_size("sp")
    chips = members // 2
    section = lax.axis_index("pipe")
    place = lax.axis_index("sp")
    core = place % 2
    chip = place // 2
    window, own_rows, width = patch_tokens.shape
    slots = window // 2
    rows = own_rows * members
    bf16 = jnp.bfloat16

    same_core = [[2 * i + c for i in range(chips)] for c in range(2)]

    def other_core(value):
        return lax.ppermute(value, "sp", [(i, i ^ 1) for i in range(members)])

    def onward(value):
        return lax.ppermute(value, "pipe", [(i, (i + 1) % sections) for i in range(sections)])

    def back(value):
        return lax.ppermute(value, "pipe", [(i, (i - 1) % sections) for i in range(sections)])

    w_before = onward(w_out[0])
    gate_before = onward(modulation[0, 0, 2:3])
    kv_own = kv_cache[0, 0]
    kv_other = other_core(kv_own)
    w_own = w_qkv[0].reshape(width, 3 * HD)
    w_other = other_core(w_own)
    mod = modulation[0, 0, 0:2]
    gain = qk_gain[0]

    to_cores = jnp.swapaxes(patch_tokens.reshape(slots, 2, own_rows, width), 0, 1)
    to_all = jnp.broadcast_to(to_cores[None], (chips, 2, slots, own_rows, width))
    entered = lax.all_to_all(
        to_all.reshape(members, slots, own_rows, width), "sp", 0, 0, tiled=True
    )
    entering = [entered[:, k].reshape(rows, width) for k in range(slots)]

    w_all = lax.all_gather(w_before, "sp", axis=0, tiled=True)

    def start_of(patch):
        chosen = jnp.sum(jnp.where(jnp.arange(order.shape[0]) == patch, order, 0))
        return jnp.sum(jnp.where(jnp.arange(offsets.shape[0]) == chosen, offsets, 0))

    starts = [start_of(2 * k + core).astype(jnp.int32) for k in range(slots)]

    ticks = sections + slots
    table = [core.astype(jnp.int32), section.astype(jnp.int32)]
    for tick in range(ticks - 1):
        start = starts[0]
        for k in range(1, slots):
            start = jnp.where(tick - section >= k, starts[k], start)
        table.append(start)
    scal = jnp.stack(table)

    statics = [mod, keep(w_own), keep(w_other), gain, keep(kv_own), keep(kv_other)]
    w_all = keep(w_all)
    hidden_shape = jax.ShapeDtypeStruct((rows, width), bf16)
    attended_shape = jax.ShapeDtypeStruct((rows, 2 * HD), bf16)
    scratch = [
        pltpu.VMEM((rows, width), bf16),
        pltpu.VMEM((2, rows, kv_own.shape[1]), jnp.float32),
    ]

    def chip_rows(hidden):
        return lax.dynamic_slice_in_dim(hidden, chip * 2 * own_rows, 2 * own_rows, 0)

    def both_patches(chip_hidden):
        first, second = chip_hidden[:own_rows], chip_hidden[own_rows:]
        mine = jnp.where(core == 0, first, second)
        theirs = other_core(jnp.where(core == 0, second, first))
        return jnp.where(core == 0, jnp.stack([mine, theirs]), jnp.stack([theirs, mine]))

    ends = jnp.where(section == 0, sections, section)
    stored = [None] * slots
    finished = [None] * slots
    hidden = entering[0]
    (attended,) = call(
        functools.partial(first_kernel, 0), [scal, hidden, *statics], (attended_shape,), scratch, True
    )
    for tick in range(1, ticks):
        arrived = onward(attended)
        arrived, hidden = lax.optimization_barrier((arrived, hidden))
        before = onward(hidden)
        gathered = lax.all_to_all(
            jnp.broadcast_to(arrived[None], (chips, rows, 2 * HD)),
            "sp", 0, 0, axis_index_groups=same_core, tiled=True,
        )
        if tick == ticks - 1:
            (hidden,) = call(
                last_kernel, [gathered, before, gate_before, w_all], (hidden_shape,), [], False
            )
        else:
            has_x = tick < slots
            extra = [entering[tick]] if has_x else []
            hidden, attended = call(
                functools.partial(whole_kernel, tick, has_x),
                [scal, gathered, before, gate_before, w_all, *extra, *statics],
                (hidden_shape, attended_shape), scratch, True,
            )
        held = chip_rows(hidden)
        for k in range(slots):
            if tick == 1 + k:
                stored[k] = held
            elif 1 + k < tick <= sections + k:
                stored[k] = jnp.where(tick == ends + k, held, stored[k])
            if tick == sections + k:
                finished[k] = both_patches(stored[k])

    section_out = jnp.concatenate([back(patches) for patches in finished])
    finished = jnp.stack(finished)

    branches = lax.axis_size("cfg")
    part = width // sections
    pieces = finished.reshape(branches, window // branches, own_rows, sections, part)
    pieces = jnp.transpose(pieces, (3, 0, 1, 2, 4))
    pieces = pieces.reshape(sections * branches, window // branches, own_rows, part)
    landed = lax.all_to_all(pieces, ("pipe", "cfg"), 0, 0, tiled=True)
    cond = landed[0].astype(jnp.float32)
    uncond = landed[1].astype(jnp.float32)
    guided = (uncond + guide_scale * (cond - uncond)).astype(bf16)
    return (section_out[None, None], guided)


def solution(mesh):
    return jax.shard_map(
        shards,
        mesh=mesh,
        in_specs=(
            P(None, "sp", None),
            P("pipe", "cfg", None, None),
            P("pipe", None, None, "sp"),
            P("pipe", None, None),
            P("pipe", "sp", None),
            P("pipe", "cfg", None, None, "sp"),
            P(),
            P(),
        ),
        out_specs=(P("pipe", "cfg", None, "sp", None), P("cfg", "sp", "pipe")),
        check_vma=False,
    )
```

```python
import functools
import math

import jax
import jax.numpy as jnp
from jax import lax
from jax.experimental import pallas as pl
from jax.experimental.pallas import tpu as pltpu
from jax.sharding import PartitionSpec as P

HD = 128
norm_eps = 1e-06
guide_scale = 3.5
CHUNK = 2048
WIDE = 512
SCALE = math.log2(math.e) / math.sqrt(HD)
VMEM_BYTES = 20 * 1024 * 1024


def dot(a, b):
    return jnp.dot(a, b, preferred_element_type=jnp.float32)


def dot_t(a, b):
    return lax.dot_general(a, b, (((1,), (1,)), ((), ())), preferred_element_type=jnp.float32)


def head_norm(heads_in, gain_row):
    power = jnp.mean(heads_in * heads_in, axis=-1, keepdims=True)
    return (heads_in * lax.rsqrt(power + norm_eps) * gain_row).astype(jnp.bfloat16)


def lanes_sum(total, wide):
    for b in range(wide.shape[1] // 128):
        total = total + wide[:, b * 128 : (b + 1) * 128]
    return total


def front_half(gathered, hidden_before, gate, w_out, hidden_out):
    rows, width = hidden_out.shape
    attended = jnp.concatenate([gathered[i] for i in range(gathered.shape[0])], axis=1)
    total = jnp.zeros((rows, 128), jnp.float32)
    for n in range(width // WIDE):
        cols = slice(n * WIDE, (n + 1) * WIDE)
        head_total = dot(attended, w_out[:, cols])
        before = hidden_before[:, cols].astype(jnp.float32)
        hidden = (before + gate[0:1, cols] * head_total).astype(jnp.bfloat16)
        hidden_out[:, cols] = hidden
        total = lanes_sum(total, hidden.astype(jnp.float32))
    return total


def back_half(
    total, hidden, modulate, w_own, w_other, gain, kv_own, kv_other, row_start, core, out, modded, scores
):
    rows, width = hidden.shape
    length = kv_own.shape[1]
    mean = jnp.sum(total, axis=1, keepdims=True) * (1.0 / width)
    spread = jnp.zeros((rows, 128), jnp.float32)
    for n in range(width // 128):
        centred = hidden[:, n * 128 : (n + 1) * 128].astype(jnp.float32) - mean
        spread = spread + centred * centred
    inverse = lax.rsqrt(jnp.sum(spread, axis=1, keepdims=True) * (1.0 / width) + norm_eps)
    for n in range(width // WIDE):
        cols = slice(n * WIDE, (n + 1) * WIDE)
        normed = (hidden[:, cols].astype(jnp.float32) - mean) * inverse
        modded[:, cols] = (normed * (1.0 + modulate[1:2, cols]) + modulate[0:1, cols]).astype(jnp.bfloat16)
    queries, fresh_keys, fresh_values = [], [], []
    for weight in (w_own, w_other):
        projected = dot(modded[...], weight[...])
        queries.append(head_norm(projected[:, :HD], gain[0:1, :]))
        fresh_keys.append(head_norm(projected[:, HD : 2 * HD], gain[1:2, :]))
        fresh_values.append(projected[:, 2 * HD :].astype(jnp.bfloat16))
    caches = (kv_own, kv_other)
    window = pl.ds(row_start, rows)
    window_block = lax.div(row_start, 128)
    steps = length // CHUNK
    lowest = jnp.full((rows, 128), -jnp.inf, jnp.float32)

    def score(head, step, top):
        part = slice(step * CHUNK, (step + 1) * CHUNK)
        old = dot_t(queries[head], caches[head][0, part, :])
        scores[:, part] = old
        for b in range(CHUNK // 128):
            replaced = step * (CHUNK // 128) + b == window_block
            top = jnp.maximum(top, jnp.where(replaced, -jnp.inf, old[:, b * 128 : (b + 1) * 128]))
        return top

    def start_weights(head, top):
        fresh = dot_t(queries[head], fresh_keys[head])
        scores[:, window] = lowest
        top = jnp.max(jnp.maximum(top, fresh), axis=1, keepdims=True)
        weights = jnp.exp2((fresh - top) * SCALE)
        return top, weights, dot(weights.astype(jnp.bfloat16), fresh_values[head])

    def weigh(head, step, top, totals, mixed):
        part = slice(step * CHUNK, (step + 1) * CHUNK)
        weights = jnp.exp2((scores[:, part] - top) * SCALE)
        totals = lanes_sum(totals, weights)
        return totals, mixed + dot(weights.astype(jnp.bfloat16), caches[head][1, part, :])

    top = lowest
    for step in range(steps):
        top = score(0, step, top)
    for head in range(2):
        top, totals, mixed = start_weights(head, top)
        next_top = lowest
        for step in range(steps):
            totals, mixed = weigh(head, step, top, totals, mixed)
            if head == 0:
                next_top = score(1, step, next_top)
        place = core if head == 0 else 1 - core
        cols = pl.ds(pl.multiple_of(place * HD, HD), HD)
        out[:, cols] = (mixed / jnp.sum(totals, axis=1, keepdims=True)).astype(jnp.bfloat16)
        top = next_top


def place_of(place, order, offsets, tick, slots):
    core = place[0]
    slot = jnp.clip(tick - place[1], 0, slots - 1)
    return core, pl.multiple_of(offsets[order[2 * slot + core]], 128)


def first_kernel(tick, slots, projects, place, order, offsets, x, *rest):
    core, row_start = place_of(place, order, offsets, tick, slots)
    weights = rest[: 2 * projects]
    mod, w_own, w_other, gain, kv_own, kv_other, out, *outs = rest[2 * projects :]
    modded, scores = outs[projects:]
    total = lanes_sum(jnp.zeros((x.shape[0], 128), jnp.float32), x[...].astype(jnp.float32))
    back_half(
        total, x, mod, w_own, w_other, gain, kv_own, kv_other,
        row_start, core, out, modded, scores,
    )
    if projects:
        parts = [out[:, pl.ds(pl.multiple_of(c * HD, HD), HD)] for c in (core, 1 - core)]
        for n in range(x.shape[1] // WIDE):
            cols = slice(n * WIDE, (n + 1) * WIDE)
            share = dot(parts[0], weights[0][:, cols]) + dot(parts[1], weights[1][:, cols])
            outs[0][:, cols] = share.astype(jnp.bfloat16)


def whole_kernel(tick, slots, place, order, offsets, gathered, before, gate, w_out, *rest):
    core, row_start = place_of(place, order, offsets, tick, slots)
    mod, w_own, w_other, gain, kv_own, kv_other, hidden, out, modded, scores = rest
    total = front_half(gathered, before, gate, w_out, hidden)
    back_half(
        total, hidden, mod, w_own, w_other, gain, kv_own, kv_other,
        row_start, core, out, modded, scores,
    )


def last_kernel(gathered, before, gate, w_out, earlier, hidden, pieces):
    front_half(gathered, before, gate, w_out, hidden)
    part = pieces.shape[3]
    for p in range(pieces.shape[0]):
        pieces[p, 0] = earlier[:, p * part : (p + 1) * part]
        pieces[p, 1] = hidden[:, p * part : (p + 1) * part]


def call(kernel, operands, outs, scratch, scalars):
    vmem = pl.BlockSpec(memory_space=pltpu.VMEM)
    smem = pl.BlockSpec(memory_space=pltpu.SMEM)
    specs = [smem] * scalars + [vmem] * (len(operands) - scalars)
    return pl.pallas_call(
        kernel,
        out_shape=outs,
        in_specs=specs,
        out_specs=tuple(vmem for _ in outs),
        scratch_shapes=scratch,
        compiler_params=pltpu.CompilerParams(vmem_limit_bytes=VMEM_BYTES),
    )(*operands)


def keep(array):
    return pltpu.with_memory_space_constraint(array, pltpu.VMEM)


def shards(patch_tokens, modulation, w_qkv, qk_gain, w_out, kv_cache, order, offsets):
    sections = lax.axis_size("pipe")
    members = lax.axis_size("sp")
    chips = members // 2
    section = lax.axis_index("pipe")
    place = lax.axis_index("sp")
    core = place % 2
    chip = place // 2
    window, own_rows, width = patch_tokens.shape
    slots = window // 2
    rows = own_rows * members
    bf16 = jnp.bfloat16

    same_core = [[2 * i + c for i in range(chips)] for c in range(2)]

    def other_core(value):
        return lax.ppermute(value, "sp", [(i, i ^ 1) for i in range(members)])

    def onward(value):
        return lax.ppermute(value, "pipe", [(i, (i + 1) % sections) for i in range(sections)])

    def back(value):
        return lax.ppermute(value, "pipe", [(i, (i - 1) % sections) for i in range(sections)])

    def gather_rows(block):
        spread = jnp.broadcast_to(block[None], (chips,) + block.shape)
        landed = lax.all_to_all(spread, "sp", 0, 0, axis_index_groups=same_core, tiled=True)
        return landed.reshape(chips * block.shape[0], block.shape[1])

    by_slot = patch_tokens.reshape(slots, 2, own_rows, width)
    to_all = jnp.broadcast_to(by_slot[0][None], (chips, 2, own_rows, width))
    entered = lax.all_to_all(
        to_all.reshape(members, own_rows, width), "sp", 0, 0, tiled=True
    ).reshape(rows, width)

    w_before = onward(w_out[0])
    gate_before = onward(modulation[0, 0, 2:3])
    kv_own = kv_cache[0, 0]
    kv_other = other_core(kv_own)
    w_own = w_qkv[0].reshape(width, 3 * HD)
    w_other = other_core(w_own)
    shares = [w_out[0], other_core(w_out[0])]
    mod = modulation[0, 0, 0:2]
    gain = qk_gain[0]

    later = jnp.where(core == 0, by_slot[1, 0], by_slot[1, 1])
    sent = other_core(jnp.where(core == 0, by_slot[1, 1], by_slot[1, 0]))
    later = jnp.where(
        core == 0, jnp.concatenate([later, sent]), jnp.concatenate([sent, later])
    )

    w_before, entered = lax.optimization_barrier((w_before, entered))
    w_all = lax.all_gather(w_before, "sp", axis=0, tiled=True)

    ticks = sections + slots
    place_here = jnp.where(jnp.arange(2) == 0, core, section).astype(jnp.int32)
    scal = [place_here, order, offsets]

    statics = [mod, keep(w_own), keep(w_other), gain, keep(kv_own), keep(kv_other)]
    w_all = keep(w_all)
    hidden_shape = jax.ShapeDtypeStruct((rows, width), bf16)
    attended_shape = jax.ShapeDtypeStruct((rows, 2 * HD), bf16)
    scratch = [
        pltpu.VMEM((rows, width), bf16),
        pltpu.VMEM((rows, kv_own.shape[1]), jnp.float32),
    ]

    def chip_rows(hidden):
        return lax.dynamic_slice_in_dim(hidden, chip * 2 * own_rows, 2 * own_rows, 0)

    def both_patches(blocks):
        first, second = blocks[:, :own_rows], blocks[:, own_rows:]
        mine = jnp.where(core == 0, first, second)
        theirs = other_core(jnp.where(core == 0, second, first))
        return jnp.where(core == 0, jnp.stack([mine, theirs], 1), jnp.stack([theirs, mine], 1))

    stored = [None] * slots
    share_shape = jax.ShapeDtypeStruct((rows, width), bf16)
    attended, share = call(
        functools.partial(first_kernel, 0, slots, 1), [*scal, entered, *shares, *statics],
        (attended_shape, share_shape), scratch, 3,
    )
    for tick in range(1, ticks):
        if tick == 1:
            landed = lax.all_to_all(
                share.reshape(chips, 2 * own_rows, width),
                "sp", 0, 0, axis_index_groups=same_core, tiled=True,
            )
            head_total = jnp.sum(landed.astype(jnp.float32), axis=0)
            gate = modulation[0, 0, 2]
            moved = onward(
                (chip_rows(entered).astype(jnp.float32) + gate * head_total).astype(bf16)
            )
            hidden = gather_rows(jnp.where(section == 0, later, moved))
            (attended,) = call(
                functools.partial(first_kernel, 1, slots, 0), [*scal, hidden, *statics],
                (attended_shape,), scratch, 3,
            )
        elif tick < ticks - 1:
            arrived = onward(attended)
            arrived, hidden = lax.optimization_barrier((arrived, hidden))
            before = onward(hidden)
            gathered = gather_rows(arrived).reshape(chips, rows, 2 * HD)
            hidden, attended = call(
                functools.partial(whole_kernel, tick, slots),
                [*scal, gathered, before, gate_before, w_all, *statics],
                (hidden_shape, attended_shape), scratch, 3,
            )
        else:
            arrived, now = lax.optimization_barrier((onward(attended), now))
            before = onward(now).reshape(2 * own_rows, width)
            gathered = lax.all_to_all(
                arrived.reshape(members, own_rows, 2 * HD), "sp", 0, 0, tiled=True
            ).reshape(chips, 2 * own_rows, 2 * HD)
            hidden, pieces = call(
                last_kernel,
                [gathered, before, gate_before, w_all, finished[0].reshape(2 * own_rows, width)],
                (
                    jax.ShapeDtypeStruct((2 * own_rows, width), bf16),
                    jax.ShapeDtypeStruct((sections, slots, 2 * own_rows, width // sections), bf16),
                ),
                [], 0,
            )
            break
        held = chip_rows(hidden)
        for k in range(slots):
            if tick == 1 + k:
                stored[k] = held
            elif 1 + k < tick < sections:
                stored[k] = jnp.where(section == tick - k, held, stored[k])
        if tick == sections:
            now, *finished = both_patches(jnp.stack([held, *stored]))
            finished[0] = jnp.where(section == 0, now, finished[0])
            finished[1] = jnp.where(section == sections - 1, now, finished[1])
            early = back(jnp.stack(finished))

    branches = lax.axis_size("cfg")
    part = width // sections
    pieces = pieces.reshape(sections * branches, 2 * own_rows, part)
    landed = lax.all_to_all(pieces, ("pipe", "cfg"), 0, 0, tiled=True)
    late = lax.ppermute(hidden, "pipe", [(0, sections - 1)]).reshape(2, own_rows, width)
    late = jnp.where(section == sections - 1, late, early[1])
    section_out = jnp.concatenate([early[0], late])
    cond = landed[0].astype(jnp.float32)
    uncond = landed[1].astype(jnp.float32)
    guided = (uncond + guide_scale * (cond - uncond)).astype(bf16)
    return (section_out[None, None], guided.reshape(2, own_rows, part))


def solution(mesh):
    return jax.shard_map(
        shards,
        mesh=mesh,
        in_specs=(
            P(None, "sp", None),
            P("pipe", "cfg", None, None),
            P("pipe", None, None, "sp"),
            P("pipe", None, None),
            P("pipe", "sp", None),
            P("pipe", "cfg", None, None, "sp"),
            P(),
            P(),
        ),
        out_specs=(P("pipe", "cfg", None, "sp", None), P("cfg", "sp", "pipe")),
        check_vma=False,
    )
```

```python
import functools
import math

import jax
import jax.numpy as jnp
from jax import lax
from jax.experimental import pallas as pl
from jax.experimental.pallas import tpu as pltpu
from jax.sharding import PartitionSpec as P

HD = 128
norm_eps = 1e-06
guide_scale = 3.5
CHUNK = 2048
WIDE = 512
SCALE = math.log2(math.e) / math.sqrt(HD)
VMEM_BYTES = 28 * 1024 * 1024
CHUNKS_BYTES = 13 * 1024 * 1024


def dot(a, b):
    return jnp.dot(a, b, preferred_element_type=jnp.float32)


def dot_t(a, b):
    return lax.dot_general(a, b, (((1,), (1,)), ((), ())), preferred_element_type=jnp.float32)


def head_norm(heads_in, gain_row):
    power = jnp.mean(heads_in * heads_in, axis=-1, keepdims=True)
    return (heads_in * lax.rsqrt(power + norm_eps) * gain_row).astype(jnp.bfloat16)


def lanes_sum(total, wide):
    for b in range(wide.shape[1] // 128):
        total = total + wide[:, b * 128 : (b + 1) * 128]
    return total


def stream(w_out, chunks, landed):
    copies = []
    for n in range(chunks.shape[0]):
        cols = slice(n * WIDE, (n + 1) * WIDE)
        copies.append(pltpu.make_async_copy(w_out.at[:, cols], chunks.at[n], landed.at[n]))
        copies[-1].start()
    return copies


def front_half(gathered, hidden_before, gate, w_out, hidden_out, chunks=None, copies=None):
    rows, width = hidden_out.shape
    attended = jnp.concatenate([gathered[i] for i in range(gathered.shape[0])], axis=1)
    total = jnp.zeros((rows, 128), jnp.float32)
    for n in range(width // WIDE):
        cols = slice(n * WIDE, (n + 1) * WIDE)
        if chunks is None:
            head_total = dot(attended, w_out[:, cols])
        else:
            copies[n].wait()
            head_total = dot(attended, chunks[n])
        before = hidden_before[:, cols].astype(jnp.float32)
        hidden = (before + gate[0:1, cols] * head_total).astype(jnp.bfloat16)
        hidden_out[:, cols] = hidden
        total = lanes_sum(total, hidden.astype(jnp.float32))
    return total


def fetch(kv_own, kv_other, caches, arrived):
    copies = {}
    for part in range(2):
        for head, kv in enumerate((kv_own, kv_other)):
            copies[head, part] = pltpu.make_async_copy(
                kv.at[part], caches.at[head, part], arrived.at[head, part]
            )
            copies[head, part].start()
    return copies


def back_half(
    total, hidden, modulate, w_own, w_other, gain, row_start, core, out, modded, scores, caches, copies
):
    rows, width = hidden.shape
    length = caches.shape[2]
    mean = jnp.sum(total, axis=1, keepdims=True) * (1.0 / width)
    spread = jnp.zeros((rows, 128), jnp.float32)
    for n in range(width // 128):
        centred = hidden[:, n * 128 : (n + 1) * 128].astype(jnp.float32) - mean
        spread = spread + centred * centred
    inverse = lax.rsqrt(jnp.sum(spread, axis=1, keepdims=True) * (1.0 / width) + norm_eps)
    for n in range(width // WIDE):
        cols = slice(n * WIDE, (n + 1) * WIDE)
        normed = (hidden[:, cols].astype(jnp.float32) - mean) * inverse
        modded[:, cols] = (normed * (1.0 + modulate[1:2, cols]) + modulate[0:1, cols]).astype(jnp.bfloat16)
    queries, fresh_keys, fresh_values = [], [], []
    for weight in (w_own, w_other):
        projected = dot(modded[...], weight[...])
        queries.append(head_norm(projected[:, :HD], gain[0:1, :]))
        fresh_keys.append(head_norm(projected[:, HD : 2 * HD], gain[1:2, :]))
        fresh_values.append(projected[:, 2 * HD :].astype(jnp.bfloat16))
    window = pl.ds(row_start, rows)
    window_block = lax.div(row_start, 128)
    steps = length // CHUNK
    lowest = jnp.full((rows, 128), -jnp.inf, jnp.float32)

    def score(head, step, top):
        part = slice(step * CHUNK, (step + 1) * CHUNK)
        old = dot_t(queries[head], caches[head, 0, part, :])
        scores[:, part] = old
        for b in range(CHUNK // 128):
            replaced = step * (CHUNK // 128) + b == window_block
            top = jnp.maximum(top, jnp.where(replaced, -jnp.inf, old[:, b * 128 : (b + 1) * 128]))
        return top

    def start_weights(head, top):
        fresh = dot_t(queries[head], fresh_keys[head])
        scores[:, window] = lowest
        top = jnp.max(jnp.maximum(top, fresh), axis=1, keepdims=True)
        weights = jnp.exp2((fresh - top) * SCALE)
        return top, weights, dot(weights.astype(jnp.bfloat16), fresh_values[head])

    def weigh(head, step, top, totals, mixed):
        part = slice(step * CHUNK, (step + 1) * CHUNK)
        weights = jnp.exp2((scores[:, part] - top) * SCALE)
        totals = lanes_sum(totals, weights)
        return totals, mixed + dot(weights.astype(jnp.bfloat16), caches[head, 1, part, :])

    top = lowest
    copies[0, 0].wait()
    for step in range(steps):
        top = score(0, step, top)
    copies[1, 0].wait()
    for head in range(2):
        copies[head, 1].wait()
        top, totals, mixed = start_weights(head, top)
        next_top = lowest
        for step in range(steps):
            totals, mixed = weigh(head, step, top, totals, mixed)
            if head == 0:
                next_top = score(1, step, next_top)
        place = core if head == 0 else 1 - core
        cols = pl.ds(pl.multiple_of(place * HD, HD), HD)
        out[:, cols] = (mixed / jnp.sum(totals, axis=1, keepdims=True)).astype(jnp.bfloat16)
        top = next_top


def place_of(place, order, offsets, tick, slots):
    core = place[0]
    slot = jnp.clip(tick - place[1], 0, slots - 1)
    return core, pl.multiple_of(offsets[order[2 * slot + core]], 128)


def first_kernel(tick, slots, projects, place, order, offsets, x, *rest):
    core, row_start = place_of(place, order, offsets, tick, slots)
    weights = rest[: 2 * projects]
    mod, w_own, w_other, gain, kv_own, kv_other, out, *outs = rest[2 * projects :]
    modded, scores, caches, arrived = outs[projects:]
    copies = fetch(kv_own, kv_other, caches, arrived)
    total = lanes_sum(jnp.zeros((x.shape[0], 128), jnp.float32), x[...].astype(jnp.float32))
    back_half(
        total, x, mod, w_own, w_other, gain, row_start, core, out, modded, scores, caches, copies
    )
    if projects:
        parts = [out[:, pl.ds(pl.multiple_of(c * HD, HD), HD)] for c in (core, 1 - core)]
        for n in range(x.shape[1] // WIDE):
            cols = slice(n * WIDE, (n + 1) * WIDE)
            share = dot(parts[0], weights[0][:, cols]) + dot(parts[1], weights[1][:, cols])
            outs[0][:, cols] = share.astype(jnp.bfloat16)


def whole_kernel(tick, slots, streams, place, order, offsets, gathered, before, gate, w_out, *rest):
    core, row_start = place_of(place, order, offsets, tick, slots)
    mod, w_own, w_other, gain, kv_own, kv_other, hidden, out, modded, scores, caches, arrived = rest[:12]
    chunks, landed = rest[12:] if streams else (None, None)
    weights = stream(w_out, chunks, landed) if streams else None
    copies = fetch(kv_own, kv_other, caches, arrived)
    total = front_half(gathered, before, gate, w_out, hidden, chunks, weights)
    back_half(
        total, hidden, mod, w_own, w_other, gain, row_start, core, out, modded, scores, caches, copies
    )


def last_kernel(w_out, gathered, before, gate, earlier, hidden, pieces, chunks, landed):
    front_half(gathered, before, gate, w_out, hidden, chunks, stream(w_out, chunks, landed))
    part = pieces.shape[3]
    for p in range(pieces.shape[0]):
        pieces[p, 0] = earlier[:, p * part : (p + 1) * part]
        pieces[p, 1] = hidden[:, p * part : (p + 1) * part]


def call(kernel, operands, outs, scratch, scalars, in_hbm):
    vmem = pl.BlockSpec(memory_space=pltpu.VMEM)
    specs = [pl.BlockSpec(memory_space=pltpu.SMEM)] * scalars + [vmem] * (len(operands) - scalars)
    for i in in_hbm:
        specs[i] = pl.BlockSpec(memory_space=pltpu.HBM)
    return pl.pallas_call(
        kernel,
        out_shape=outs,
        in_specs=specs,
        out_specs=tuple(vmem for _ in outs),
        scratch_shapes=scratch,
        compiler_params=pltpu.CompilerParams(
            vmem_limit_bytes=VMEM_BYTES + (CHUNKS_BYTES if len(scratch) > 4 else 0)
        ),
    )(*operands)


def keep(array):
    return pltpu.with_memory_space_constraint(array, pltpu.VMEM)


def shards(patch_tokens, modulation, w_qkv, qk_gain, w_out, kv_cache, order, offsets):
    sections = lax.axis_size("pipe")
    members = lax.axis_size("sp")
    chips = members // 2
    section = lax.axis_index("pipe")
    place = lax.axis_index("sp")
    core = place % 2
    chip = place // 2
    window, own_rows, width = patch_tokens.shape
    slots = window // 2
    rows = own_rows * members
    bf16 = jnp.bfloat16

    same_core = [[2 * i + c for i in range(chips)] for c in range(2)]

    def other_core(value):
        return lax.ppermute(value, "sp", [(i, i ^ 1) for i in range(members)])

    def onward(value):
        return lax.ppermute(value, "pipe", [(i, (i + 1) % sections) for i in range(sections)])

    def back(value):
        return lax.ppermute(value, "pipe", [(i, (i - 1) % sections) for i in range(sections)])

    def gather_rows(block):
        spread = jnp.broadcast_to(block[None], (chips,) + block.shape)
        landed = lax.all_to_all(spread, "sp", 0, 0, axis_index_groups=same_core, tiled=True)
        return landed.reshape(chips * block.shape[0], block.shape[1])

    by_slot = patch_tokens.reshape(slots, 2, own_rows, width)
    to_all = jnp.broadcast_to(by_slot[0][None], (chips, 2, own_rows, width))
    entered = lax.all_to_all(
        to_all.reshape(members, own_rows, width), "sp", 0, 0, tiled=True
    ).reshape(rows, width)

    w_before = onward(w_out[0])
    gate_before = onward(modulation[0, 0, 2:3])
    other_share, kv_own = lax.optimization_barrier((other_core(w_out[0]), kv_cache[0, 0]))
    shares = [w_out[0], other_share]
    kv_other = other_core(kv_own)
    w_own = w_qkv[0].reshape(width, 3 * HD)
    w_other = other_core(w_own)
    mod = modulation[0, 0, 0:2]
    gain = qk_gain[0]

    later = jnp.where(core == 0, by_slot[1, 0], by_slot[1, 1])
    sent = other_core(jnp.where(core == 0, by_slot[1, 1], by_slot[1, 0]))
    later = jnp.where(
        core == 0, jnp.concatenate([later, sent]), jnp.concatenate([sent, later])
    )

    w_before, entered = lax.optimization_barrier((w_before, entered))
    w_all = lax.all_gather(w_before, "sp", axis=0, tiled=True)

    ticks = sections + slots
    place_here = jnp.where(jnp.arange(2) == 0, core, section).astype(jnp.int32)
    scal = [place_here, order, offsets]

    statics = [mod, keep(w_own), keep(w_other), gain, kv_own, kv_other]
    hidden_shape = jax.ShapeDtypeStruct((rows, width), bf16)
    attended_shape = jax.ShapeDtypeStruct((rows, 2 * HD), bf16)
    scratch = [
        pltpu.VMEM((rows, width), bf16),
        pltpu.VMEM((rows, kv_own.shape[1]), jnp.float32),
        pltpu.VMEM((2,) + kv_own.shape, bf16),
        pltpu.SemaphoreType.DMA((2, 2)),
    ]
    chunked = [
        pltpu.VMEM((width // WIDE, w_all.shape[0], WIDE), bf16),
        pltpu.SemaphoreType.DMA((width // WIDE,)),
    ]
    caches_at = [-2, -1]

    def chip_rows(hidden):
        return lax.dynamic_slice_in_dim(hidden, chip * 2 * own_rows, 2 * own_rows, 0)

    def both_patches(blocks):
        first, second = blocks[:, :own_rows], blocks[:, own_rows:]
        mine = jnp.where(first_core, first, second)
        theirs = other_core(jnp.where(first_core, second, first))
        return jnp.where(first_core, jnp.stack([mine, theirs], 1), jnp.stack([theirs, mine], 1))

    share_shape = jax.ShapeDtypeStruct((rows, width), bf16)
    attended, share = call(
        functools.partial(first_kernel, 0, slots, 1), [*scal, entered, *shares, *statics],
        (attended_shape, share_shape), scratch, 3, caches_at,
    )
    base = lax.dynamic_slice_in_dim(entered, chip * 2 * own_rows, 2 * own_rows, 0)
    gate = modulation[0, 0, 2]
    masks = [section == q for q in range(sections)]
    share, base, gate, later, gate_before, masks, first_core = lax.optimization_barrier(
        (share, base, gate, later, gate_before, masks, core == 0)
    )
    stored = [later] * slots
    for tick in range(1, ticks):
        if tick == 1:
            landed = lax.all_to_all(
                share.reshape(chips, 2 * own_rows, width),
                "sp", 0, 0, axis_index_groups=same_core, tiled=True,
            )
            head_total = jnp.sum(landed.astype(jnp.float32), axis=0)
            moved = onward((base.astype(jnp.float32) + gate * head_total).astype(bf16))
            hidden = gather_rows(jnp.where(masks[0], later, moved))
            (attended,) = call(
                functools.partial(first_kernel, 1, slots, 0), [*scal, hidden, *statics],
                (attended_shape,), scratch, 3, caches_at,
            )
        elif tick < ticks - 1:
            arrived = onward(attended)
            arrived, hidden = lax.optimization_barrier((arrived, hidden))
            before = onward(hidden)
            gathered = gather_rows(arrived).reshape(chips, rows, 2 * HD)
            streams = tick == 2
            hidden, attended = call(
                functools.partial(whole_kernel, tick, slots, streams),
                [*scal, gathered, before, gate_before, w_all if streams else keep(w_all), *statics],
                (hidden_shape, attended_shape),
                scratch + (chunked if streams else []), 3, caches_at + [6] * streams,
            )
        else:
            arrived, now = lax.optimization_barrier((onward(attended), now))
            before = onward(now).reshape(2 * own_rows, width)
            gathered = lax.all_to_all(
                arrived.reshape(members, own_rows, 2 * HD), "sp", 0, 0, tiled=True
            ).reshape(chips, 2 * own_rows, 2 * HD)
            hidden, pieces = call(
                last_kernel,
                [w_all, gathered, before, gate_before, finished[0].reshape(2 * own_rows, width)],
                (
                    jax.ShapeDtypeStruct((2 * own_rows, width), bf16),
                    jax.ShapeDtypeStruct((sections, slots, 2 * own_rows, width // sections), bf16),
                ),
                chunked, 0, [0],
            )
            break
        held = chip_rows(hidden)
        for k in range(slots):
            if tick == 1 + k:
                stored[k] = held
            elif 1 + k < tick < sections:
                stored[k] = jnp.where(masks[tick - k], held, stored[k])
        attended, hidden, stored = lax.optimization_barrier((attended, hidden, stored))
        if tick == sections:
            now, *finished = both_patches(jnp.stack([held, *stored]))
            finished[0] = jnp.where(masks[0], now, finished[0])
            finished[1] = jnp.where(masks[-1], now, finished[1])
            early = back(jnp.stack(finished))

    branches = lax.axis_size("cfg")
    part = width // sections
    pieces = pieces.reshape(sections * branches, 2 * own_rows, part)
    landed = lax.all_to_all(pieces, ("pipe", "cfg"), 0, 0, tiled=True)
    late = lax.ppermute(hidden, "pipe", [(0, sections - 1)]).reshape(2, own_rows, width)
    late = jnp.where(masks[-1], late, early[1])
    section_out = jnp.concatenate([early[0], late])
    cond = landed[0].astype(jnp.float32)
    uncond = landed[1].astype(jnp.float32)
    guided = (uncond + guide_scale * (cond - uncond)).astype(bf16)
    return (section_out[None, None], guided.reshape(2, own_rows, part))


def solution(mesh):
    return jax.shard_map(
        shards,
        mesh=mesh,
        in_specs=(
            P(None, "sp", None),
            P("pipe", "cfg", None, None),
            P("pipe", None, None, "sp"),
            P("pipe", None, None),
            P("pipe", "sp", None),
            P("pipe", "cfg", None, None, "sp"),
            P(),
            P(),
        ),
        out_specs=(P("pipe", "cfg", None, "sp", None), P("cfg", "sp", "pipe")),
        check_vma=False,
    )
```
